32 devices in a mesh: head: 8 (over z, core), seq: 4 (over y, x).
Axes of the slice: x: 2, y: 2, z: 4, core: 2. Of those that a mesh axis runs over, the one named last changes fastest.
Arguments:
- queries: bfloat16 [8, 8192, 64], P('head', 'seq'), may hold values from -160 to 160
- keys: bfloat16 [8, 8192, 64], P('head', 'seq'), may hold values from -8 to 8
- values: bfloat16 [8, 8192, 64], P('head', 'seq'), may hold values from -20 to 20
- block_mask: int32 [8, 16, 64], P('head'), may hold values from 0 to 1, as said below
- block_order: int32 [16], replicated, may hold values from 0 to 15, as said below
- sparse_gain: float32 [8, 64], P('head'), may hold values from 0.1 to 1.9
- linear_gain: float32 [8, 64], P('head'), may hold values from 0.1 to 1.9
Outputs:
- mixed: float32 [8, 8192, 64], P('head', 'seq')
The draws below stay inside these ranges and needn't reach their ends.
Inputs may be any that keep to these rules, and one draw needn't show every extreme that they name: A permutation of the query blocks; rows b * 512 to (b + 1) * 512 - 1 of queries and mixed belong to query block block_order[b]. Each row block_mask[h, n] has exactly 6 ones; at most 2 of them lie among the 16 key blocks of one index of seq, and in every row some index holds exactly 2; key block n * 4 is always selected by query block n.
All inputs are finite; a program needn't handle non-finite values.
Results may differ from the reference program's by a relative error of at most 0.002.
Values may be sent and summed in bfloat16 or wider, within the bound.
A program may use at most 64 MiB of HBM per device.

```python
import jax
import jax.numpy as jnp
from jax import lax

DH = 64
BQ = 512
BK = 128
HEADS = 8
TOKENS = 8192
KB_DEV = 16
NQB = 16
KEYSPAN_GROUPS = 64
SEL = 6
CAP = 2
N_SEQ = 4


def order_for(key):
    return jax.random.permutation(jax.random.fold_in(key, 101), NQB).astype(jnp.int32)


def keys_for(key):
    shape = (HEADS, TOKENS, DH)
    base = jax.random.normal(jax.random.fold_in(key, 102), shape, jnp.float32)
    return jnp.clip(base, -8.0, 8.0)


def draw_block_order(key, part):
    return order_for(key)


def draw_keys(key, part):
    return keys_for(key).astype(jnp.bfloat16)


def draw_queries(key, part):
    shape = (HEADS, TOKENS, DH)
    base = jax.random.normal(jax.random.fold_in(key, 105), shape, jnp.float32)
    return jnp.clip(base, -160.0, 160.0).astype(jnp.bfloat16)


def draw_values(key, part):
    shape = (HEADS, TOKENS, DH)
    head_ids = jnp.arange(HEADS, dtype=jnp.float32)
    rising = 3.0 ** (head_ids / max(HEADS - 1, 1))
    jitter = jnp.exp(jax.random.uniform(jax.random.fold_in(key, 108), (HEADS,), jnp.float32, -0.2, 0.2))
    base = jax.random.normal(jax.random.fold_in(key, 109), shape, jnp.float32)
    scaled = base * (rising * jitter)[:, None, None]
    return jnp.clip(scaled, -20.0, 20.0).astype(jnp.bfloat16)


def row_ranks(row_key):
    return jax.random.permutation(row_key, KEYSPAN_GROUPS)


def draw_block_mask(key, part):
    row_keys = jax.random.split(jax.random.fold_in(key, 112), HEADS * NQB)
    tile_ordinals = jax.vmap(row_ranks)(row_keys).reshape(HEADS, NQB, KEYSPAN_GROUPS).astype(jnp.int32)
    preferred_tiles = jax.random.randint(jax.random.fold_in(key, 113), (HEADS, NQB, 1), 0, N_SEQ).astype(jnp.int32)
    block_ids = jnp.arange(KEYSPAN_GROUPS, dtype=jnp.int32)
    accelerator_table = block_ids // KB_DEV
    own_first = (jnp.arange(NQB, dtype=jnp.int32) * BQ // BK)[:, None]
    relevance_increment = KEYSPAN_GROUPS * (accelerator_table[None, None, :] == preferred_tiles).astype(jnp.int32)
    mandatory_tiles = 2 * KEYSPAN_GROUPS * (block_ids[None, :] == own_first).astype(jnp.int32)
    tile_relevance = tile_ordinals + relevance_increment + mandatory_tiles[None, :, :]
    grouped = tile_relevance.reshape(HEADS, NQB, N_SEQ, KB_DEV)
    best, places = lax.top_k(grouped, CAP)
    candidate_ids = places + (jnp.arange(N_SEQ, dtype=jnp.int32) * KB_DEV)[None, None, :, None]
    flat_scores = best.reshape(HEADS, NQB, N_SEQ * CAP)
    flat_ids = candidate_ids.reshape(HEADS, NQB, N_SEQ * CAP)
    unused, chosen = lax.top_k(flat_scores, SEL)
    chosen_ids = jnp.take_along_axis(flat_ids, chosen, axis=2)
    return jnp.sum((chosen_ids[..., None] == block_ids).astype(jnp.int32), axis=2)


def setup_inputs(seed: int = 0) -> dict:
    arg_keys = jax.random.split(jax.random.key(seed), 8)
    return {
        "queries": draw_queries(jax.random.fold_in(arg_keys[7], 71), 0),
        "keys": draw_keys(jax.random.fold_in(arg_keys[7], 71), 0),
        "values": draw_values(jax.random.fold_in(arg_keys[7], 71), 0),
        "block_mask": draw_block_mask(jax.random.fold_in(arg_keys[7], 71), 0),
        "block_order": draw_block_order(jax.random.fold_in(arg_keys[7], 71), 0),
        "sparse_gain": jnp.clip(1.0 + 0.18 * jax.random.normal(arg_keys[5], (HEADS, DH), jnp.float32), 0.1, 1.9),
        "linear_gain": jnp.clip(1.0 + 0.18 * jax.random.normal(arg_keys[6], (HEADS, DH), jnp.float32), 0.1, 1.9),
    }


EPSILON = 1e-06
TOP_PRECISION = lax.Precision.HIGHEST

def feature(values_in):
    return jax.nn.elu(values_in) + 1.0

def head_branches(inputs):
    query_head, key_head, value_head, mask_rows = inputs
    feat_keys = feature(key_head.astype(jnp.float32)).reshape(KEYSPAN_GROUPS, BK, DH)
    value_blocks = value_head.astype(jnp.float32).reshape(KEYSPAN_GROUPS, BK, DH)
    states = jnp.einsum('jtd,jte->jde', feat_keys, value_blocks, precision=TOP_PRECISION).reshape(KEYSPAN_GROUPS, DH * DH)
    key_sums = lax.optimization_barrier(jnp.sum(feat_keys, axis=1))
    unselected = 1.0 - mask_rows.astype(jnp.float32)
    remaining_states = jnp.dot(unselected, states, precision=TOP_PRECISION).reshape(NQB, DH, DH)
    remaining_sums = jnp.dot(unselected, key_sums, precision=TOP_PRECISION)
    feature_query = feature(query_head.astype(jnp.float32)).reshape(NQB, BQ, DH)
    numerator = jnp.einsum('svo,sol->svl', feature_query, remaining_states, precision=TOP_PRECISION)
    denominator = jnp.einsum('ryh,rh->ry', feature_query, remaining_sums, precision=TOP_PRECISION)
    linear = (numerator / denominator[:, :, None]).reshape(TOKENS, DH)
    key_blocks = key_head.astype(jnp.float32).reshape(KEYSPAN_GROUPS, BK, DH)
    query_blocks = query_head.astype(jnp.float32).reshape(NQB, BQ, DH)

    def sparse_block(block_item):
        query_block, mask_row = block_item
        chosen = jnp.argsort(1 - mask_row, stable=True)[:SEL]
        keys_chosen = key_blocks[chosen].reshape(SEL * BK, DH)
        values_chosen = value_blocks[chosen].reshape(SEL * BK, DH)
        tile_relevance = jnp.dot(query_block, keys_chosen.T, precision=TOP_PRECISION) * DH ** (-0.5)
        row_top = lax.optimization_barrier(jnp.max(tile_relevance, axis=1, keepdims=True))
        weights = jnp.exp(tile_relevance - row_top)
        row_total = lax.optimization_barrier(jnp.sum(weights, axis=1, keepdims=True))
        rounded = lax.optimization_barrier(weights.astype(jnp.bfloat16)).astype(jnp.float32)
        return jnp.dot(rounded, values_chosen, precision=TOP_PRECISION) / row_total
    sparse = lax.map(sparse_block, (query_blocks, mask_rows)).reshape(TOKENS, DH)
    return (sparse, linear)

def reference(queries, keys, values, block_mask, block_order, sparse_gain, linear_gain):
    ordered = jnp.take(block_mask, block_order.astype(jnp.int32), axis=1)
    sparse, linear = lax.map(head_branches, (queries, keys, values, ordered))
    features = HEADS * DH
    rms_sparse = jnp.sqrt(lax.optimization_barrier(jnp.sum(sparse * sparse, axis=(0, 2))) / features + EPSILON)
    rms_linear = jnp.sqrt(lax.optimization_barrier(jnp.sum(linear * linear, axis=(0, 2))) / features + EPSILON)
    first = sparse / rms_sparse[None, :, None] * sparse_gain[:, None, :]
    second = linear / rms_linear[None, :, None] * linear_gain[:, None, :]
    return first + second
```

```python
import functools

import jax
import jax.numpy as jnp
from jax import lax
from jax.experimental import pallas as pl
from jax.experimental.pallas import tpu as pltpu
from jax.sharding import PartitionSpec as P

BQ = 512
BK = 128
SLOTS = 2
EPSILON = 1e-06
NEGATIVE = -1e30
MESH = pl.DeviceIdType.MESH


def phi(x):
    return jnp.where(x > 0, x + 1.0, jnp.exp(jnp.minimum(x, 0.0)))


def pack(pick_ref, k_ref, v_ref, out_ref):
    n_seq, n_query = out_ref.shape[:2]

    @pl.loop(0, n_seq)
    def _(dev):
        for b in range(n_query):
            for s in range(SLOTS):
                block = pick_ref[(dev * n_query + b) * SLOTS + s]
                columns = pl.ds(pl.multiple_of(block * BK, BK), BK)
                out_ref[dev, b, 0, :, s * BK : (s + 1) * BK] = k_ref[:, columns]
                out_ref[dev, b, 1, :, s * BK : (s + 1) * BK] = v_ref[:, columns]


def kernel(
    n_seq, n_head, n_query, n_key, features,
    bias_ref, send, q_ref, k_ref, v_ref, coef_ref, gain_ref, out_ref,
    recv, usend, urecv, states, scores, sq, linear_ref, sparse_ref,
    kv_send_sem, kv_recv_sem, u_send_sem, u_recv_sem, sq_send_sem, sq_recv_sem,
):
    me = lax.axis_index("seq")
    head = lax.axis_index("head")
    width = q_ref.shape[0]
    rows = usend.shape[2]
    pairs = n_query // 2

    def peer(o):
        return lax.rem(me + o, n_seq)

    def head_peer(o):
        return lax.rem(head + o, n_head)

    def kv_copy(dev, at, b):
        return pltpu.make_async_remote_copy(
            src_ref=send.at[dev, b], dst_ref=recv.at[at, b],
            send_sem=kv_send_sem.at[dev, b], recv_sem=kv_recv_sem.at[at, b],
            device_id={"seq": dev}, device_id_type=MESH,
        )

    def u_copy(dev, at):
        return pltpu.make_async_remote_copy(
            src_ref=usend.at[dev], dst_ref=urecv.at[at],
            send_sem=u_send_sem.at[dev], recv_sem=u_recv_sem.at[at],
            device_id={"seq": dev}, device_id_type=MESH,
        )

    def sq_copy(dev, at, b):
        return pltpu.make_async_remote_copy(
            src_ref=sq.at[head, b], dst_ref=sq.at[at, b],
            send_sem=sq_send_sem.at[dev, b], recv_sem=sq_recv_sem.at[at, b],
            device_id={"head": dev}, device_id_type=MESH,
        )

    barrier = pltpu.get_barrier_semaphore()

    @pl.loop(1, n_seq)
    def _(o):
        pl.semaphore_signal(barrier, inc=1, device_id={"seq": peer(o)}, device_id_type=MESH)

    @pl.loop(1, n_head)
    def _(o):
        pl.semaphore_signal(barrier, inc=1, device_id={"head": head_peer(o)}, device_id_type=MESH)

    pl.semaphore_wait(barrier, n_seq + n_head - 2)
    for b in range(n_query):

        @pl.loop(1, n_seq)
        def _(o):
            kv_copy(peer(o), me, b).start()

    ones = jnp.ones((16, BK), jnp.bfloat16)
    for j in range(n_key):
        columns = slice(j * BK, (j + 1) * BK)
        feat = phi(k_ref[:, columns].astype(jnp.float32))
        feat = jnp.concatenate([feat, feat], axis=0)
        high = feat.astype(jnp.bfloat16)
        low = (feat - high.astype(jnp.float32)).astype(jnp.bfloat16)
        wide = jnp.concatenate([v_ref[:, columns], ones], axis=0)
        dims = (((1,), (1,)), ((), ()))
        state = lax.dot_general(wide, high, dims, preferred_element_type=jnp.float32)
        state += lax.dot_general(wide, low, dims, preferred_element_type=jnp.float32)
        states[j] = state[:rows]

    def combine(dev, target, place):
        for p in range(pairs):
            total = jnp.zeros((rows, 2 * width), jnp.float32)
            for j in range(n_key):
                total += states[j] * coef_ref[dev * pairs + p, j : j + 1, :]
            target[place, p] = total

    @pl.loop(1, n_seq)
    def _(o):
        combine(peer(o), usend, peer(o))
        u_copy(peer(o), me).start()

    combine(me, urecv, me)
    recv[me] = send[me]

    @pl.loop(1, n_seq)
    def _(o):
        u_copy(peer(o), peer(o)).wait_recv()

    def sums(x):
        total = jnp.sum(x * x, axis=0, keepdims=True)
        return [total[:, i * BK : (i + 1) * BK] for i in range(BQ // BK)]

    @pl.loop(0, pairs)
    def _(p):
        state = urecv[0, p]
        for src in range(1, n_seq):
            state += urecv[src, p]
        for half in range(2):
            b = p * 2 + half
            here = pl.ds(pl.multiple_of(b * BQ, BQ), BQ)
            query = q_ref[:, here].astype(jnp.float32)
            mine = jnp.dot(
                state[:, half * width : (half + 1) * width], phi(query),
                preferred_element_type=jnp.float32, precision=lax.Precision.HIGH,
            )
            linear = mine[:width] / mine[width : width + 1]
            linear_ref[:, here] = linear
            scaled = (query * width ** (-0.5)).astype(jnp.bfloat16)

            @pl.loop(1, n_seq)
            def _(o):
                kv_copy(peer(o), peer(o), b).wait_recv()

            top = jnp.full((1, BQ), NEGATIVE, jnp.float32)
            for src in range(n_seq):
                part = lax.dot_general(
                    recv[src, b, 0], scaled, (((0,), (0,)), ((), ())),
                    preferred_element_type=jnp.float32,
                )
                for s in range(SLOTS):
                    one = part[s * BK : (s + 1) * BK] + bias_ref[(b * n_seq + src) * SLOTS + s]
                    scores[src, s * BK : (s + 1) * BK] = one
                    top = jnp.maximum(top, jnp.max(one, axis=0, keepdims=True))
            total = jnp.zeros((1, BQ), jnp.float32)
            acc = jnp.zeros((width, BQ), jnp.float32)
            for src in range(n_seq):
                weights = jnp.exp(scores[src] - top)
                total += jnp.sum(weights, axis=0, keepdims=True)
                acc += jnp.dot(
                    recv[src, b, 1], weights.astype(jnp.bfloat16),
                    preferred_element_type=jnp.float32,
                )
            sparse = acc / total
            sparse_ref[:, here] = sparse
            sq[head, b] = jnp.concatenate(sums(sparse) + sums(linear), axis=0)

            @pl.loop(1, n_head)
            def _(o):
                sq_copy(head_peer(o), head, b).start()

    gain_sparse = gain_ref[:, 0:1]
    gain_linear = gain_ref[:, 1:2]

    @pl.loop(0, n_query)
    def _(b):
        @pl.loop(1, n_head)
        def _(o):
            sq_copy(head_peer(o), head_peer(o), b).wait_recv()

        total = sq[0, b]
        for h in range(1, n_head):
            total += sq[h, b]
        scale = 1.0 / jnp.sqrt(total / features + EPSILON)
        parts = BQ // BK
        for i in range(parts):
            here = pl.ds(pl.multiple_of(b * BQ + i * BK, BK), BK)
            first = sparse_ref[:, here] * scale[i : i + 1] * gain_sparse
            second = linear_ref[:, here] * scale[parts + i : parts + i + 1] * gain_linear
            out_ref[:, here] = first + second

    @pl.loop(1, n_seq)
    def _(o):
        u_copy(peer(o), me).wait_send()
        for b in range(n_query):
            kv_copy(peer(o), me, b).wait_send()

    @pl.loop(1, n_head)
    def _(o):
        for b in range(n_query):
            sq_copy(head_peer(o), head, b).wait_send()


def body(queries, keys, values, block_mask, block_order, sparse_gain, linear_gain):
    tokens, width = queries.shape[1:]
    n_seq, n_head = lax.axis_size("seq"), lax.axis_size("head")
    me = lax.axis_index("seq")
    n_query, n_key = tokens // BQ, tokens // BK
    positions = block_order.shape[0]
    pairs = n_query // 2
    hot = block_order[:, None] == jnp.arange(positions, dtype=jnp.int32)[None, :]
    ordered = jnp.sum(jnp.where(hot[:, :, None], block_mask[0][None], 0), axis=1)
    local = lax.dynamic_slice_in_dim(ordered, me * n_key, n_key, 1)
    own = lax.dynamic_slice_in_dim(ordered, me * n_query, n_query, 0)
    column = jnp.arange(n_key, dtype=jnp.int32)[None, :]
    first = jnp.min(jnp.where(local > 0, column, n_key), axis=1)
    last = jnp.max(jnp.where(local > 0, column, 0), axis=1)
    pick = jnp.stack([jnp.minimum(first, n_key - 1), last], axis=1).reshape(-1)
    count = jnp.sum(own.reshape(n_query, n_seq, n_key), axis=2)
    slot = jnp.arange(SLOTS, dtype=jnp.int32)
    bias = jnp.where(slot < count[:, :, None], 0.0, NEGATIVE).astype(jnp.float32).reshape(-1)
    open_blocks = 1.0 - local.astype(jnp.float32)
    coef = open_blocks.reshape(n_seq * pairs, 2, n_key).swapaxes(1, 2)
    coef = jnp.repeat(coef, width, axis=2)
    gains = jnp.concatenate([sparse_gain, linear_gain], axis=0).T
    rows = width + 8
    vmem = pl.BlockSpec(memory_space=pltpu.VMEM)
    smem = pl.BlockSpec(memory_space=pltpu.SMEM)
    dma = pltpu.SemaphoreType.DMA
    packed = pl.pallas_call(
        pack,
        out_shape=jax.ShapeDtypeStruct(
            (n_seq, n_query, 2, width, SLOTS * BK), jnp.bfloat16
        ),
        in_specs=[smem, vmem, vmem],
        out_specs=vmem,
        compiler_params=pltpu.CompilerParams(vmem_limit_bytes=24 * 1024 * 1024),
    )(pick, keys[0].T, values[0].T)
    out = pl.pallas_call(
        functools.partial(
            kernel, n_seq, n_head, n_query, n_key, n_head * queries.shape[0] * width
        ),
        out_shape=jax.ShapeDtypeStruct((width, tokens), jnp.float32),
        in_specs=[smem] + [vmem] * 6,
        out_specs=vmem,
        scratch_shapes=[
            pltpu.VMEM((n_seq, n_query, 2, width, SLOTS * BK), jnp.bfloat16),
            pltpu.VMEM((n_seq, pairs, rows, 2 * width), jnp.float32),
            pltpu.VMEM((n_seq, pairs, rows, 2 * width), jnp.float32),
            pltpu.VMEM((n_key, rows, 2 * width), jnp.float32),
            pltpu.VMEM((n_seq, SLOTS * BK, BQ), jnp.float32),
            pltpu.VMEM((n_head, n_query, 2 * (BQ // BK), BK), jnp.float32),
            pltpu.VMEM((width, tokens), jnp.float32),
            pltpu.VMEM((width, tokens), jnp.float32),
            dma((n_seq, n_query)), dma((n_seq, n_query)),
            dma((n_seq,)), dma((n_seq,)),
            dma((n_head, n_query)), dma((n_head, n_query)),
        ],
        compiler_params=pltpu.CompilerParams(
            collective_id=0, has_side_effects=True, vmem_limit_bytes=44 * 1024 * 1024
        ),
    )(bias, packed, queries[0].T, keys[0].T, values[0].T, coef, gains)
    return out.T[None]


def solution(mesh):
    in_specs = (
        P("head", "seq", None),
        P("head", "seq", None),
        P("head", "seq", None),
        P("head", None, None),
        P(),
        P("head", None),
        P("head", None),
    )
    out_specs = P("head", "seq", None)
    return jax.shard_map(body, mesh=mesh, in_specs=in_specs, out_specs=out_specs, check_vma=False)
```

```python
import functools

import jax
import jax.numpy as jnp
from jax import lax
from jax.experimental import pallas as pl
from jax.experimental.pallas import tpu as pltpu
from jax.sharding import PartitionSpec as P

BQ = 512
BK = 128
SLOTS = 2
EPSILON = 1e-06
NEGATIVE = -1e30
MESH = pl.DeviceIdType.MESH


def phi(x):
    return jnp.where(x > 0, x + 1.0, jnp.exp(jnp.minimum(x, 0.0)))


def pack(pick_ref, k_ref, v_ref, out_ref):
    n_seq, n_query = out_ref.shape[:2]

    @pl.loop(0, n_seq)
    def _(dev):
        for b in range(n_query):
            for s in range(SLOTS):
                block = pick_ref[(dev * n_query + b) * SLOTS + s]
                columns = pl.ds(pl.multiple_of(block * BK, BK), BK)
                out_ref[dev, b, 0, :, s * BK : (s + 1) * BK] = k_ref[:, columns]
                out_ref[dev, b, 1, :, s * BK : (s + 1) * BK] = v_ref[:, columns]


def kernel(
    n_seq, n_head, n_query, n_key, features,
    bias_ref, open_ref, send, q_ref, k_ref, v_ref, gain_sparse_ref, gain_linear_ref, out_ref,
    recv, usend, urecv, states, scores, sq, linear_ref, sparse_ref,
    kv_send_sem, kv_recv_sem, u_send_sem, u_recv_sem, sq_send_sem, sq_recv_sem,
):
    me = lax.axis_index("seq")
    head = lax.axis_index("head")
    width = q_ref.shape[0]
    rows = usend.shape[2]
    pairs = n_query // 2

    def peer(o):
        return lax.rem(me + o, n_seq)

    def head_peer(o):
        return lax.rem(head + o, n_head)

    def kv_copy(dev, at, b):
        return pltpu.make_async_remote_copy(
            src_ref=send.at[dev, b], dst_ref=recv.at[at, b],
            send_sem=kv_send_sem.at[dev, b], recv_sem=kv_recv_sem.at[at, b],
            device_id={"seq": dev}, device_id_type=MESH,
        )

    def u_copy(dev, at):
        return pltpu.make_async_remote_copy(
            src_ref=usend.at[dev], dst_ref=urecv.at[at],
            send_sem=u_send_sem.at[dev], recv_sem=u_recv_sem.at[at],
            device_id={"seq": dev}, device_id_type=MESH,
        )

    def sq_copy(dev, at, b):
        return pltpu.make_async_remote_copy(
            src_ref=sq.at[head, b], dst_ref=sq.at[at, b],
            send_sem=sq_send_sem.at[dev, b], recv_sem=sq_recv_sem.at[at, b],
            device_id={"head": dev}, device_id_type=MESH,
        )

    barrier = pltpu.get_barrier_semaphore()

    @pl.loop(1, n_seq)
    def _(o):
        pl.semaphore_signal(barrier, inc=1, device_id={"seq": peer(o)}, device_id_type=MESH)

    @pl.loop(1, n_head)
    def _(o):
        pl.semaphore_signal(barrier, inc=1, device_id={"head": head_peer(o)}, device_id_type=MESH)

    ones = jnp.ones((16, BK), jnp.bfloat16)
    for j in range(n_key):
        columns = slice(j * BK, (j + 1) * BK)
        feat = phi(k_ref[:, columns].astype(jnp.float32))
        feat = jnp.concatenate([feat, feat], axis=0)
        high = feat.astype(jnp.bfloat16)
        low = (feat - high.astype(jnp.float32)).astype(jnp.bfloat16)
        wide = jnp.concatenate([v_ref[:, columns], ones], axis=0)
        dims = (((1,), (1,)), ((), ()))
        state = lax.dot_general(wide, high, dims, preferred_element_type=jnp.float32)
        state += lax.dot_general(wide, low, dims, preferred_element_type=jnp.float32)
        states[j] = state[:rows]

    low_half = lax.broadcasted_iota(jnp.int32, (1, 2 * width), 1) < width

    def combine(dev, target, place):
        for p in range(pairs):
            total = jnp.zeros((rows, 2 * width), jnp.float32)
            at = dev * n_query + 2 * p
            for j in range(n_key):
                total += states[j] * jnp.where(low_half, open_ref[at, j], open_ref[at + 1, j])
            target[place, p] = total

    @pl.loop(1, n_seq)
    def _(o):
        combine(peer(o), usend, peer(o))

    pl.semaphore_wait(barrier, n_seq + n_head - 2)

    def send_blocks(b):
        @pl.loop(1, n_seq)
        def _(o):
            kv_copy(peer(o), me, b).start()

    send_blocks(0)

    @pl.loop(1, n_seq)
    def _(o):
        u_copy(peer(o), me).start()

    for b in range(1, n_query):
        send_blocks(b)

    combine(me, urecv, me)
    recv[me] = send[me]

    def span(b):
        return pl.ds(pl.multiple_of(b * BQ, BQ), BQ)

    def attend(b):
        scaled = (q_ref[:, span(b)].astype(jnp.float32) * width ** (-0.5)).astype(jnp.bfloat16)

        @pl.loop(1, n_seq)
        def _(o):
            kv_copy(peer(o), peer(o), b).wait_recv()

        top = jnp.full((1, BQ), NEGATIVE, jnp.float32)
        for src in range(n_seq):
            part = lax.dot_general(
                recv[src, b, 0], scaled, (((0,), (0,)), ((), ())),
                preferred_element_type=jnp.float32,
            )
            for s in range(SLOTS):
                one = part[s * BK : (s + 1) * BK] + bias_ref[b, src * SLOTS + s]
                scores[src, s * BK : (s + 1) * BK] = one
                top = jnp.maximum(top, jnp.max(one, axis=0, keepdims=True))
        total = jnp.zeros((1, BQ), jnp.float32)
        acc = jnp.zeros((width, BQ), jnp.float32)
        for src in range(n_seq):
            weights = jnp.exp(scores[src] - top)
            total += jnp.sum(weights, axis=0, keepdims=True)
            acc += jnp.dot(
                recv[src, b, 1], weights.astype(jnp.bfloat16),
                preferred_element_type=jnp.float32,
            )
        sparse_ref[:, span(b)] = acc * (1.0 / total)

    def attend_linear():
        for p in range(pairs):
            state = urecv[0, p]
            for src in range(1, n_seq):
                state += urecv[src, p]
            for half in range(2):
                b = p * 2 + half
                mine = jnp.dot(
                    state[:, half * width : (half + 1) * width],
                    phi(q_ref[:, b * BQ : (b + 1) * BQ].astype(jnp.float32)),
                    preferred_element_type=jnp.float32, precision=lax.Precision.HIGH,
                )
                linear_ref[:, b * BQ : (b + 1) * BQ] = mine[:width] * (1.0 / mine[width : width + 1])

    def sums(x):
        total = jnp.sum(x * x, axis=0, keepdims=True)
        return [total[:, i * BK : (i + 1) * BK] for i in range(BQ // BK)]

    def share(b):
        sq[head, b] = jnp.concatenate(
            sums(sparse_ref[:, span(b)]) + sums(linear_ref[:, span(b)]), axis=0
        )

        @pl.loop(1, n_head)
        def _(o):
            sq_copy(head_peer(o), head, b).start()

    diagonal = lax.broadcasted_iota(jnp.int32, (width, width), 0) == lax.broadcasted_iota(
        jnp.int32, (width, width), 1
    )
    gain_sparse = jnp.sum(jnp.where(diagonal, gain_sparse_ref[...], 0.0), axis=1, keepdims=True)
    gain_linear = jnp.sum(jnp.where(diagonal, gain_linear_ref[...], 0.0), axis=1, keepdims=True)

    def finish(b):
        @pl.loop(1, n_head)
        def _(o):
            sq_copy(head_peer(o), head_peer(o), b).wait_recv()

        total = sq[0, b]
        for h in range(1, n_head):
            total += sq[h, b]
        scale = 1.0 / jnp.sqrt(total / features + EPSILON)
        parts = BQ // BK
        for i in range(parts):
            here = pl.ds(pl.multiple_of(b * BQ + i * BK, BK), BK)
            first = sparse_ref[:, here] * scale[i : i + 1] * gain_sparse
            second = linear_ref[:, here] * scale[parts + i : parts + i + 1] * gain_linear
            out_ref[:, here] = first + second

    attend(0)

    @pl.loop(1, n_seq)
    def _(o):
        u_copy(peer(o), peer(o)).wait_recv()

    attend_linear()
    share(0)

    @pl.loop(1, n_query)
    def _(b):
        attend(b)
        share(b)
        finish(b - 1)

    finish(n_query - 1)

    @pl.loop(1, n_seq)
    def _(o):
        u_copy(peer(o), me).wait_send()
        for b in range(n_query):
            kv_copy(peer(o), me, b).wait_send()

    @pl.loop(1, n_head)
    def _(o):
        for b in range(n_query):
            sq_copy(head_peer(o), head, b).wait_send()


def body(queries, keys, values, block_mask, block_order, sparse_gain, linear_gain):
    tokens, width = queries.shape[1:]
    n_seq, n_head = lax.axis_size("seq"), lax.axis_size("head")
    me = lax.axis_index("seq")
    n_query, n_key = tokens // BQ, tokens // BK
    positions = block_order.shape[0]
    pairs = n_query // 2
    hot = block_order[:, None] == jnp.arange(positions, dtype=jnp.int32)[None, :]
    ordered = jnp.sum(jnp.where(hot[:, :, None], block_mask[0][None], 0), axis=1)
    local = lax.dynamic_slice_in_dim(ordered, me * n_key, n_key, 1)
    own = lax.dynamic_slice_in_dim(ordered, me * n_query, n_query, 0)
    column = jnp.arange(n_key, dtype=jnp.int32)[None, :]
    first = jnp.min(jnp.where(local > 0, column, n_key), axis=1)
    last = jnp.max(jnp.where(local > 0, column, 0), axis=1)
    pick = jnp.stack([jnp.minimum(first, n_key - 1), last], axis=1).reshape(-1)
    count = jnp.sum(own.reshape(n_query, n_seq, n_key), axis=2)
    slot = jnp.arange(SLOTS, dtype=jnp.int32)
    bias = jnp.where(slot < count[:, :, None], 0.0, NEGATIVE).astype(jnp.float32).reshape(n_query, -1)
    opened = 1.0 - local.astype(jnp.float32)
    rows = width + 8
    vmem = pl.BlockSpec(memory_space=pltpu.VMEM)
    smem = pl.BlockSpec(memory_space=pltpu.SMEM)
    dma = pltpu.SemaphoreType.DMA
    packed = pl.pallas_call(
        pack,
        out_shape=jax.ShapeDtypeStruct(
            (n_seq, n_query, 2, width, SLOTS * BK), jnp.bfloat16
        ),
        in_specs=[smem, vmem, vmem],
        out_specs=vmem,
        compiler_params=pltpu.CompilerParams(vmem_limit_bytes=24 * 1024 * 1024),
    )(pick, keys[0].T, values[0].T)
    out = pl.pallas_call(
        functools.partial(
            kernel, n_seq, n_head, n_query, n_key, n_head * queries.shape[0] * width
        ),
        out_shape=jax.ShapeDtypeStruct((width, tokens), jnp.float32),
        in_specs=[smem, smem] + [vmem] * 6,
        out_specs=vmem,
        scratch_shapes=[
            pltpu.VMEM((n_seq, n_query, 2, width, SLOTS * BK), jnp.bfloat16),
            pltpu.VMEM((n_seq, pairs, rows, 2 * width), jnp.float32),
            pltpu.VMEM((n_seq, pairs, rows, 2 * width), jnp.float32),
            pltpu.VMEM((n_key, rows, 2 * width), jnp.float32),
            pltpu.VMEM((n_seq, SLOTS * BK, BQ), jnp.float32),
            pltpu.VMEM((n_head, n_query, 2 * (BQ // BK), BK), jnp.float32),
            pltpu.VMEM((width, tokens), jnp.float32),
            pltpu.VMEM((width, tokens), jnp.float32),
            dma((n_seq, n_query)), dma((n_seq, n_query)),
            dma((n_seq,)), dma((n_seq,)),
            dma((n_head, n_query)), dma((n_head, n_query)),
        ],
        compiler_params=pltpu.CompilerParams(
            collective_id=0, has_side_effects=True, vmem_limit_bytes=44 * 1024 * 1024
        ),
    )(
        bias, opened, packed, queries[0].T, keys[0].T, values[0].T, sparse_gain, linear_gain
    )
    return out.T[None]


def solution(mesh):
    in_specs = (
        P("head", "seq", None),
        P("head", "seq", None),
        P("head", "seq", None),
        P("head", None, None),
        P(),
        P("head", None),
        P("head", None),
    )
    out_specs = P("head", "seq", None)
    return jax.shard_map(body, mesh=mesh, in_specs=in_specs, out_specs=out_specs, check_vma=False)
```

```python
import functools

import jax
import jax.numpy as jnp
from jax import lax
from jax.experimental import pallas as pl
from jax.experimental.pallas import tpu as pltpu
from jax.sharding import PartitionSpec as P

BQ = 512
BK = 128
SLOTS = 2
EPSILON = 1e-06
NEGATIVE = -1e30
MESH = pl.DeviceIdType.MESH


def phi(x):
    return jnp.where(x > 0, x + 1.0, jnp.exp(jnp.minimum(x, 0.0)))


def pack(first_ref, last_ref, k_ref, v_ref, out_ref):
    n_seq, n_query = out_ref.shape[:2]

    @pl.loop(0, n_seq)
    def _(dev):
        for b in range(n_query):
            for s, pick_ref in enumerate((first_ref, last_ref)):
                block = pick_ref[dev * n_query + b]
                columns = pl.ds(pl.multiple_of(block * BK, BK), BK)
                out_ref[dev, b, 0, :, s * BK : (s + 1) * BK] = k_ref[:, columns]
                out_ref[dev, b, 1, :, s * BK : (s + 1) * BK] = v_ref[:, columns]


def kernel(
    n_seq, n_head, n_query, n_key, features,
    bias_ref, open_ref, send, q_ref, k_ref, v_ref, gain_sparse_ref, gain_linear_ref, out_ref,
    recv, usend, urecv, states, scores, sq, linear_ref, sparse_ref,
    kv_send_sem, kv_recv_sem, u_send_sem, u_recv_sem, sq_send_sem, sq_recv_sem,
):
    me = lax.axis_index("seq")
    head = lax.axis_index("head")
    width = q_ref.shape[0]
    rows = usend.shape[2]
    pairs = n_query // 2

    def peer(o):
        return lax.rem(me + o, n_seq)

    def head_peer(o):
        return lax.rem(head + o, n_head)

    def kv_copy(dev, at, b):
        return pltpu.make_async_remote_copy(
            src_ref=send.at[dev, b], dst_ref=recv.at[at, b],
            send_sem=kv_send_sem.at[dev, b], recv_sem=kv_recv_sem.at[at, b],
            device_id={"seq": dev}, device_id_type=MESH,
        )

    def u_copy(dev, at):
        return pltpu.make_async_remote_copy(
            src_ref=usend.at[dev], dst_ref=urecv.at[at],
            send_sem=u_send_sem.at[dev], recv_sem=u_recv_sem.at[at],
            device_id={"seq": dev}, device_id_type=MESH,
        )

    def sq_copy(dev, at, b):
        return pltpu.make_async_remote_copy(
            src_ref=sq.at[head, b], dst_ref=sq.at[at, b],
            send_sem=sq_send_sem.at[dev, b], recv_sem=sq_recv_sem.at[at, b],
            device_id={"head": dev}, device_id_type=MESH,
        )

    barrier = pltpu.get_barrier_semaphore()

    @pl.loop(1, n_seq)
    def _(o):
        pl.semaphore_signal(barrier, inc=1, device_id={"seq": peer(o)}, device_id_type=MESH)

    @pl.loop(1, n_head)
    def _(o):
        pl.semaphore_signal(barrier, inc=1, device_id={"head": head_peer(o)}, device_id_type=MESH)

    ones = jnp.ones((16, BK), jnp.bfloat16)
    for j in range(n_key):
        columns = slice(j * BK, (j + 1) * BK)
        feat = phi(k_ref[:, columns].astype(jnp.float32))
        feat = jnp.concatenate([feat, feat], axis=0)
        high = feat.astype(jnp.bfloat16)
        low = (feat - high.astype(jnp.float32)).astype(jnp.bfloat16)
        wide = jnp.concatenate([v_ref[:, columns], ones], axis=0)
        dims = (((1,), (1,)), ((), ()))
        state = lax.dot_general(wide, high, dims, preferred_element_type=jnp.float32)
        state += lax.dot_general(wide, low, dims, preferred_element_type=jnp.float32)
        states[j] = state[:rows]

    low_half = lax.broadcasted_iota(jnp.int32, (1, 2 * width), 1) < width

    def combine(dev, target, place):
        for p in range(pairs):
            total = jnp.zeros((rows, 2 * width), jnp.float32)
            at = dev * n_query + 2 * p
            for j in range(n_key):
                total += states[j] * jnp.where(low_half, open_ref[at, j], open_ref[at + 1, j])
            target[place, p] = total

    @pl.loop(1, n_seq)
    def _(o):
        combine(peer(o), usend, peer(o))

    pl.semaphore_wait(barrier, n_seq + n_head - 2)

    def send_blocks(b):
        @pl.loop(1, n_seq)
        def _(o):
            kv_copy(peer(o), me, b).start()

    send_blocks(0)

    @pl.loop(1, n_seq)
    def _(o):
        u_copy(peer(o), me).start()

    for b in range(1, n_query):
        send_blocks(b)

    combine(me, urecv, me)
    recv[me] = send[me]

    def span(b):
        return pl.ds(pl.multiple_of(b * BQ, BQ), BQ)

    def attend(b):
        scaled = (q_ref[:, span(b)].astype(jnp.float32) * width ** (-0.5)).astype(jnp.bfloat16)

        @pl.loop(1, n_seq)
        def _(o):
            kv_copy(peer(o), peer(o), b).wait_recv()

        top = jnp.full((1, BQ), NEGATIVE, jnp.float32)
        for src in range(n_seq):
            part = lax.dot_general(
                recv[src, b, 0], scaled, (((0,), (0,)), ((), ())),
                preferred_element_type=jnp.float32,
            )
            for s in range(SLOTS):
                one = part[s * BK : (s + 1) * BK] + bias_ref[b, src * SLOTS + s]
                scores[src, s * BK : (s + 1) * BK] = one
                top = jnp.maximum(top, jnp.max(one, axis=0, keepdims=True))
        total = jnp.zeros((1, BQ), jnp.float32)
        acc = jnp.zeros((width, BQ), jnp.float32)
        for src in range(n_seq):
            weights = jnp.exp(scores[src] - top)
            total += jnp.sum(weights, axis=0, keepdims=True)
            acc += jnp.dot(
                recv[src, b, 1], weights.astype(jnp.bfloat16),
                preferred_element_type=jnp.float32,
            )
        sparse_ref[:, span(b)] = acc * (1.0 / total)

    def attend_linear():
        for p in range(pairs):
            state = urecv[0, p]
            for src in range(1, n_seq):
                state += urecv[src, p]
            for half in range(2):
                b = p * 2 + half
                mine = jnp.dot(
                    state[:, half * width : (half + 1) * width],
                    phi(q_ref[:, b * BQ : (b + 1) * BQ].astype(jnp.float32)),
                    preferred_element_type=jnp.float32, precision=lax.Precision.HIGH,
                )
                linear_ref[:, b * BQ : (b + 1) * BQ] = mine[:width] * (1.0 / mine[width : width + 1])

    def sums(x):
        total = jnp.sum(x * x, axis=0, keepdims=True)
        return [total[:, i * BK : (i + 1) * BK] for i in range(BQ // BK)]

    def share(b):
        sq[head, b] = jnp.concatenate(
            sums(sparse_ref[:, span(b)]) + sums(linear_ref[:, span(b)]), axis=0
        )

        @pl.loop(1, n_head)
        def _(o):
            sq_copy(head_peer(o), head, b).start()

    diagonal = lax.broadcasted_iota(jnp.int32, (width, width), 0) == lax.broadcasted_iota(
        jnp.int32, (width, width), 1
    )
    gain_sparse = jnp.sum(jnp.where(diagonal, gain_sparse_ref[...], 0.0), axis=1, keepdims=True)
    gain_linear = jnp.sum(jnp.where(diagonal, gain_linear_ref[...], 0.0), axis=1, keepdims=True)

    def finish(b):
        @pl.loop(1, n_head)
        def _(o):
            sq_copy(head_peer(o), head_peer(o), b).wait_recv()

        total = sq[0, b]
        for h in range(1, n_head):
            total += sq[h, b]
        scale = 1.0 / jnp.sqrt(total / features + EPSILON)
        parts = BQ // BK
        for i in range(parts):
            here = pl.ds(pl.multiple_of(b * BQ + i * BK, BK), BK)
            first = sparse_ref[:, here] * scale[i : i + 1] * gain_sparse
            second = linear_ref[:, here] * scale[parts + i : parts + i + 1] * gain_linear
            out_ref[:, here] = first + second

    attend(0)

    @pl.loop(1, n_seq)
    def _(o):
        u_copy(peer(o), peer(o)).wait_recv()

    attend_linear()
    share(0)

    @pl.loop(1, n_query)
    def _(b):
        attend(b)
        share(b)
        finish(b - 1)

    finish(n_query - 1)

    @pl.loop(1, n_seq)
    def _(o):
        u_copy(peer(o), me).wait_send()
        for b in range(n_query):
            kv_copy(peer(o), me, b).wait_send()

    @pl.loop(1, n_head)
    def _(o):
        for b in range(n_query):
            sq_copy(head_peer(o), head, b).wait_send()


def body(queries, keys, values, block_mask, block_order, sparse_gain, linear_gain):
    tokens, width = queries.shape[1:]
    n_seq, n_head = lax.axis_size("seq"), lax.axis_size("head")
    me = lax.axis_index("seq")
    n_query, n_key = tokens // BQ, tokens // BK
    positions = block_order.shape[0]
    pairs = n_query // 2
    hot = block_order[:, None] == jnp.arange(positions, dtype=jnp.int32)[None, :]
    ordered = jnp.sum(jnp.where(hot[:, :, None], block_mask[0][None], 0), axis=1)
    local = lax.dynamic_slice_in_dim(ordered, me * n_key, n_key, 1)
    own = lax.dynamic_slice_in_dim(ordered, me * n_query, n_query, 0)
    column = jnp.arange(n_key, dtype=jnp.int32)[None, :]
    first = jnp.min(jnp.where(local > 0, column, n_key), axis=1)
    last = jnp.max(jnp.where(local > 0, column, 0), axis=1)
    first = jnp.minimum(first, n_key - 1)
    count = jnp.sum(own.reshape(n_query, n_seq, n_key), axis=2)
    slot = jnp.arange(SLOTS, dtype=jnp.int32)
    bias = jnp.where(slot < count[:, :, None], 0.0, NEGATIVE).astype(jnp.float32).reshape(n_query, -1)
    opened = 1.0 - local.astype(jnp.float32)
    rows = width + 8
    vmem = pl.BlockSpec(memory_space=pltpu.VMEM)
    smem = pl.BlockSpec(memory_space=pltpu.SMEM)
    dma = pltpu.SemaphoreType.DMA
    packed = pl.pallas_call(
        pack,
        out_shape=jax.ShapeDtypeStruct(
            (n_seq, n_query, 2, width, SLOTS * BK), jnp.bfloat16
        ),
        in_specs=[smem, smem, vmem, vmem],
        out_specs=vmem,
        compiler_params=pltpu.CompilerParams(vmem_limit_bytes=24 * 1024 * 1024),
    )(first, last, keys[0].T, values[0].T)
    out = pl.pallas_call(
        functools.partial(
            kernel, n_seq, n_head, n_query, n_key, n_head * queries.shape[0] * width
        ),
        out_shape=jax.ShapeDtypeStruct((width, tokens), jnp.float32),
        in_specs=[smem, smem] + [vmem] * 6,
        out_specs=vmem,
        scratch_shapes=[
            pltpu.VMEM((n_seq, n_query, 2, width, SLOTS * BK), jnp.bfloat16),
            pltpu.VMEM((n_seq, pairs, rows, 2 * width), jnp.float32),
            pltpu.VMEM((n_seq, pairs, rows, 2 * width), jnp.float32),
            pltpu.VMEM((n_key, rows, 2 * width), jnp.float32),
            pltpu.VMEM((n_seq, SLOTS * BK, BQ), jnp.float32),
            pltpu.VMEM((n_head, n_query, 2 * (BQ // BK), BK), jnp.float32),
            pltpu.VMEM((width, tokens), jnp.float32),
            pltpu.VMEM((width, tokens), jnp.float32),
            dma((n_seq, n_query)), dma((n_seq, n_query)),
            dma((n_seq,)), dma((n_seq,)),
            dma((n_head, n_query)), dma((n_head, n_query)),
        ],
        compiler_params=pltpu.CompilerParams(
            collective_id=0, has_side_effects=True, vmem_limit_bytes=44 * 1024 * 1024
        ),
    )(
        bias, opened, packed, queries[0].T, keys[0].T, values[0].T, sparse_gain, linear_gain
    )
    return out.T[None]


def solution(mesh):
    in_specs = (
        P("head", "seq", None),
        P("head", "seq", None),
        P("head", "seq", None),
        P("head", None, None),
        P(),
        P("head", None),
        P("head", None),
    )
    out_specs = P("head", "seq", None)
    return jax.shard_map(body, mesh=mesh, in_specs=in_specs, out_specs=out_specs, check_vma=False)
```
